256 devices in a mesh: aux: 32 (over x, y, core), basis: 8 (over z).
Axes of the slice: x: 4, y: 4, z: 8, core: 2. Of those that a mesh axis runs over, the one named last changes fastest.
Arguments:
- integrals: bfloat16 [96, 24, 32, 4096], P('basis', None, 'aux'), may hold values from -6 to 6
- coefficients: bfloat16 [6144, 1280], P('aux'), may hold values from -0.119628906 to 0.119628906
- block_nu: int32 [96, 24], P('basis'), may hold values from 0 to 95, as said below
- block_count: int32 [96], P('basis'), may hold values from 6 to 24, as said below
Outputs:
- occupied_integrals: float32 [32, 1280, 1280], P(None, 'aux', 'basis')
The draws below stay inside these ranges and needn't reach their ends.
Inputs may be any that keep to these rules, and one draw needn't show every extreme that they name: `block_nu`: the nu blocks of one mu block's slots are distinct. Slots from block_count on are ignored, whatever their integrals hold; in every group of 12 consecutive mu blocks some mu block has all 24 slots live.
All inputs are finite; a program needn't handle non-finite values.
Results may differ from the reference program's by a relative error of at most 0.0029.
Values may be sent and summed in bfloat16 or wider, within the bound.
A program may use at most 128 MiB of HBM per device.

```python
import jax
import jax.numpy as jnp
from jax import lax

BLK = 64
NBF = 6144
NOCC = 1280
KMAX = 24
AUX = 32
MUB = 12


def draw_block_nu(key, part):
    key = jax.random.fold_in(key, 11)
    block_keys = jax.random.split(key, NBF // BLK)

    def one_block(single):
        return jax.random.permutation(single, NBF // BLK)[:KMAX]
    return jax.vmap(one_block)(block_keys).astype(jnp.int32)


def draw_block_count(key, part):
    key = jax.random.fold_in(key, 23)
    live_counts = jax.random.randint(key, (NBF // BLK,), (KMAX + 3) // 4, KMAX + 1)
    groups = NBF // BLK // MUB
    full_block = jax.random.randint(jax.random.fold_in(key, 1), (groups,), 0, MUB)
    marker = jnp.arange(MUB, dtype=jnp.int32)[None, :] == full_block[:, None]
    live_counts = jnp.where(marker, KMAX, live_counts.reshape(groups, MUB))
    return live_counts.reshape(-1).astype(jnp.int32)


def block_levels(key, extent, cuts, smallest, top_value):
    def one(dim, blocks):
        heights = jax.random.uniform(jax.random.fold_in(jax.random.fold_in(key, 6), dim), (blocks,), jnp.float32, smallest / len(cuts), top_value / len(cuts))
        return jnp.repeat(jnp.exp(heights), extent[dim] // blocks).reshape((-1,) + (1,) * (len(extent) - dim - 1))

    gain = one(*cuts[0])
    for cut in cuts[1:]:
        gain = gain * one(*cut)
    return gain


def scatter_about(own_key, shape, width, reach, cuts=(), held_as=jnp.bfloat16):
    array = jax.random.normal(own_key, shape, jnp.float32) * width
    if len(cuts) > 0:
        array = block_levels(own_key, shape, cuts, -0.22, 0.18) * array
    return jnp.clip(array, min=-reach, max=reach).astype(held_as)


def setup_inputs(seed: int = 0) -> dict:
    streams_of = jax.random.split(jax.random.key(seed), 5)
    return {
        "integrals": scatter_about(streams_of[0], (NBF // BLK, KMAX, AUX, BLK * BLK), 1.0, 6.0, ((0, 8), (2, 32))),
        "coefficients": scatter_about(streams_of[1], (NBF, NOCC), 0.02, 0.119628906, ((0, 32),)),
        "block_nu": draw_block_nu(jax.random.fold_in(streams_of[4], 71), 0),
        "block_count": draw_block_count(jax.random.fold_in(streams_of[4], 71), 0),
    }


def reference(integrals, coefficients, block_nu, block_count):
    mu_total, slot_count, aux_total, block_area = integrals.shape
    occupied = coefficients.shape[1]
    offsets = jnp.arange(BLK, dtype=jnp.int32)
    row_coeffs = coefficients.reshape(mu_total, BLK, occupied).astype(jnp.float32)

    def transform(unused_state, slot_data):
        blocks, nu_ids, live_count = slot_data
        row_index = (nu_ids[:, None] * BLK + offsets[None, :]).reshape(-1).astype(jnp.int32)
        picked = jnp.take(coefficients, row_index, axis=0).reshape(slot_count, BLK, occupied).astype(jnp.float32)
        live_slots = (jnp.arange(slot_count, dtype=jnp.int32) < live_count).astype(jnp.float32)
        masked = blocks.reshape(slot_count, -1, BLK, BLK).astype(jnp.float32) * live_slots[:, None, None, None]
        half_block = jnp.einsum("kpab,kbi->pai", masked, picked)
        return unused_state, half_block.astype(jnp.bfloat16)

    def one_group(start):
        aux_slab = lax.dynamic_slice_in_dim(integrals, start, 8, 2)
        unused_state, halves = lax.scan(transform, jnp.float32(0), (aux_slab, block_nu, block_count))
        return jnp.einsum("mpai,maj->pij", halves.astype(jnp.float32), row_coeffs)

    result = lax.map(one_group, jnp.arange(0, aux_total, 8, dtype=jnp.int32))
    return result.reshape(aux_total, occupied, occupied)
```

```python
import functools

import jax
import jax.numpy as jnp
from jax import lax
from jax.experimental import pallas as pl
from jax.experimental.pallas import tpu as pltpu
from jax.sharding import PartitionSpec as P

BLK = 64
SIDE = 4
MESH = pl.DeviceIdType.MESH


def relayout(raw, count, target, m, first_row):
    slots, area = raw.shape[1:]
    values = raw[m].astype(jnp.float32)
    slot_ids = lax.broadcasted_iota(jnp.int32, (slots, area), 0)
    values = jnp.where(slot_ids < count, values, 0.0)
    pairs = area // (2 * BLK)
    by_pair = jnp.stack([values[:, 2 * BLK * a : 2 * BLK * (a + 1)] for a in range(pairs)], axis=0)
    by_slot = jnp.swapaxes(by_pair, 0, 1)
    low = lax.broadcasted_iota(jnp.int32, (pairs, 2 * BLK), 1) < BLK
    for k in range(0, slots, 2):
        one, two = by_slot[k], by_slot[k + 1]
        even = jnp.where(low, one, pltpu.roll(two, BLK, 1))
        odd = jnp.where(low, pltpu.roll(one, BLK, 1), two)
        columns = slice(BLK * k, BLK * (k + 2))
        target[m, pl.ds(first_row, pairs), columns] = even.astype(jnp.bfloat16)
        target[m, pl.ds(first_row + pairs, pairs), columns] = odd.astype(jnp.bfloat16)


def turned(blocks, first_block):
    new = lax.broadcasted_iota(jnp.int32, (BLK, BLK), 1)
    old = lax.broadcasted_iota(jnp.int32, (BLK, BLK), 0)
    source = jnp.where(new < BLK // 2, 2 * new, 2 * new - BLK + 1)
    order = (old == source).astype(jnp.bfloat16)
    columns = [
        lax.dot_general(
            blocks[first_block + m], order, (((0,), (0,)), ((), ())), preferred_element_type=jnp.float32
        )
        for m in range(12)
    ]
    return jnp.concatenate(columns, axis=1).astype(jnp.bfloat16)


def kernel(
    depth, integrals, shard, block_nu, block_count, out,
    raw, coef, mats, other, turned_rows, half, outgoing, incoming, final, flipped, landed,
    local_sems, send_sems, recv_sems, last_send, last_recv,
):
    me = lax.axis_index("aux")
    z = lax.axis_index("basis")
    core = lax.rem(me, 2)
    chip = lax.div(me, 2)
    x = lax.div(chip, SIDE)
    y = lax.rem(chip, SIDE)
    width = coef.shape[2]
    mu_blocks = raw.shape[0]
    group = 6

    def device(dx, dy, dz=0, core_at=core):
        at_x = lax.rem(x + dx + SIDE, SIDE)
        at_y = lax.rem(y + dy + SIDE, SIDE)
        return ((at_x * SIDE + at_y) * 2 + core_at, lax.rem(z + dz + depth, depth))

    partner = device(0, 0, 0, 1 - core)

    fetch = pltpu.make_async_copy(integrals, raw, local_sems.at[0])
    fetch.start()
    mine = coef.at[pl.ds(group * chip + 3 * core, 3)]
    keep = pltpu.make_async_copy(
        shard.at[:, :, pl.ds(pl.multiple_of(width * core, 128), width)], mine, local_sems.at[1]
    )
    keep.start()

    barrier = pltpu.get_barrier_semaphore()
    for friend in (
        device(1, 0), device(-1, 0), device(0, 1), device(0, -1), device(0, 0, 1), device(0, 0, -1), partner,
    ):
        pl.semaphore_signal(barrier, inc=1, device_id=friend, device_id_type=MESH)
    sender_core = lax.div(me, 16)

    @pl.loop(0, 16)
    def _(s):
        sender = 2 * s + sender_core

        @pl.when(sender != me)
        def _():
            pl.semaphore_signal(barrier, inc=1, device_id=(sender, z), device_id_type=MESH)

    pl.semaphore_wait(barrier, jnp.where(sender_core == core, 7 + 15, 7 + 16))

    copies = []

    def send(src, dst, target):
        k = len(copies)
        copy = pltpu.make_async_remote_copy(
            src_ref=src, dst_ref=dst, send_sem=send_sems.at[k], recv_sem=recv_sems.at[k],
            device_id=target, device_id_type=MESH,
        )
        copy.start()
        copies.append(copy)
        return copy

    swap = send(shard.at[:, :, pl.ds(pl.multiple_of(width * (1 - core), 128), width)], mine, partner)
    keep.wait()
    swap.wait_recv()

    parity = lax.rem(z, 2)

    class Stream:
        def __init__(self, offset, along_x, up):
            self.offset, self.along_x, self.up = offset, along_x, up
            self.plus, self.minus, self.far = {}, {}, {}

        def device(self, df, dg):
            return device(df, dg) if self.along_x else device(dg, df)

        def block(self, df, dg):
            dx, dy = (df, dg) if self.along_x else (dg, df)
            at_x = lax.rem(x + dx + SIDE, SIDE)
            at_y = lax.rem(y + dy + SIDE, SIDE)
            return coef.at[group * (at_x * SIDE + at_y) + self.offset]

        def first(self):
            block = self.block(0, 0)
            self.first_plus = send(block, block, self.device(1, 0))
            self.first_minus = send(block, block, self.device(-1, 0))

        def first_on(self):
            self.first_plus.wait_recv()
            low = self.block(-1, 0).at[pl.ds(0, BLK // 2)]
            self.far_low = send(low, low, self.device(1, 0))
            self.first_minus.wait_recv()
            high = self.block(1, 0).at[pl.ds(BLK // 2, BLK // 2)]
            self.far_high = send(high, high, self.device(-1, 0))

        def first_end(self):
            self.far_low.wait_recv()
            self.far_high.wait_recv()

        def second(self, df):
            block = self.block(df, 0)
            self.plus[df] = send(block, block, self.device(0, 1))
            self.minus[df] = send(block, block, self.device(0, -1))

        def second_on(self, df):
            self.plus[df].wait_recv()
            low = self.block(df, -1).at[pl.ds(0, BLK // 2)]
            low_copy = send(low, low, self.device(0, 1))
            self.minus[df].wait_recv()
            high = self.block(df, 1).at[pl.ds(BLK // 2, BLK // 2)]
            self.far[df] = (low_copy, send(high, high, self.device(0, -1)))

        def second_end(self, df):
            for copy in self.far[df]:
                copy.wait_recv()

        def beside(self, df, dg):
            if self.up:
                block = self.block(df, dg)
                from_beside.append(send(block, block, device(0, 0, self.up)))

    from_beside = []
    streams = [
        Stream(2 + 2 * parity, True, 1),
        Stream(3 + 2 * parity, False, -1),
        Stream(0, True, 0),
        Stream(1, False, 0),
    ]
    fetched = [False]

    def bring(begin, end):
        if not fetched[0]:
            fetch.wait()
            fetched[0] = True

        @pl.loop(begin, end)
        def _(m):
            relayout(raw, block_count[m], mats, m, pl.multiple_of(BLK * core, BLK))

        part = mats.at[pl.ds(begin, end - begin), pl.ds(pl.multiple_of(BLK * core, BLK), BLK)]
        return send(part, part, partner)

    for stream in streams:
        stream.first()
    for stream in streams[:2]:
        stream.second(0)
    mats_in = [bring(0, 4)]
    for stream in streams:
        stream.first_on()
    for stream in streams:
        stream.beside(-1, 0)
        stream.beside(1, 0)
    for stream in streams[2:]:
        stream.second(0)
    for stream in streams:
        stream.second(-1)
        stream.second(1)
    for stream in streams:
        stream.first_end()
        stream.second(2)
        stream.beside(2, 0)
    mats_in.append(bring(4, 8))
    before = None
    for df in (0, -1, 1, 2):
        for stream in streams:
            stream.second_on(df)
            stream.beside(df, -1)
            stream.beside(df, 1)
            if before is not None:
                stream.second_end(before)
                stream.beside(before, 2)
        if before is None:
            mats_in.append(bring(8, 12))
        before = df
    for stream in streams:
        stream.second_end(before)
        stream.beside(before, 2)
    for copy in from_beside:
        copy.wait_recv()

    own_first = mu_blocks * z
    other_in = send(coef.at[pl.ds(own_first, mu_blocks)], other, partner)
    per_core = 4

    def place(rows, at_core):
        for q in range(per_core):
            turned_rows[per_core * at_core + q] = rows[160 * q : 160 * (q + 1)]

    place(turned(coef, own_first), core)
    for copy in mats_in:
        copy.wait_recv()

    @pl.loop(0, mu_blocks)
    def _(m):
        picked = jnp.concatenate([coef[block_nu[m, k]] for k in range(raw.shape[1])], axis=0)
        product = jnp.dot(mats[m], picked, preferred_element_type=jnp.float32)
        rows = pl.ds(pl.multiple_of(m * BLK, BLK), BLK)
        half[0, rows, :] = product[:BLK].astype(jnp.bfloat16)
        half[1, rows, :] = product[BLK:].astype(jnp.bfloat16)

    other_in.wait_recv()
    place(turned(other, 0), 1 - core)

    def partial_sum(target, p):
        return jnp.dot(turned_rows[target], half[p], preferred_element_type=jnp.float32)

    steps = 7
    ring = [[], []]
    for k in range(steps):
        distance = 4 - (k + 1) // 2
        for way in range(2):
            p = k % 2 if way == 0 else 1 - k % 2
            step = distance if way == 0 else -distance
            value = partial_sum(lax.rem(z + step + depth, depth), p)
            if k >= 2:
                ring[way][k - 2].wait_recv()
                value = value + incoming[way, k - 2].astype(jnp.float32)
            outgoing[way, k] = value.astype(jnp.bfloat16)
            ring[way].append(
                send(outgoing.at[way, k], incoming.at[way, k], device(0, 0, 1 if way == 0 else -1))
            )
    own = [partial_sum(z, p) for p in range(2)]
    for way in range(2):
        for k in (5, 6):
            ring[way][k].wait_recv()
    for p in range(2):
        up, down = (6, 5) if p == 0 else (5, 6)
        value = own[p] + incoming[0, up].astype(jnp.float32) + incoming[1, down].astype(jnp.float32)
        final[128 * p : 128 * (p + 1), :] = value[:128]
        final[256 + 32 * p : 256 + 32 * (p + 1), :] = value[128:]
    final[320:384, :] = jnp.zeros((64, width), jnp.float32)
    flipped[...] = jnp.transpose(final[...], (1, 0))

    @pl.loop(0, 16)
    def _(i):
        t = lax.rem(chip + i, 16)
        owner = 16 * core + t
        src = flipped.at[pl.ds(pl.multiple_of(40 * t, 8), 40)]

        @pl.when(owner == me)
        def _():
            pltpu.make_async_copy(src, landed.at[chip], last_recv.at[chip]).start()

        @pl.when(owner != me)
        def _():
            pltpu.make_async_remote_copy(
                src_ref=src, dst_ref=landed.at[chip], send_sem=last_send.at[t], recv_sem=last_recv.at[chip],
                device_id=(owner, z), device_id_type=MESH,
            ).start()

    for s in range(16):
        pltpu.make_async_copy(landed.at[s], landed.at[s], last_recv.at[s]).wait()
        for p in range(2):
            out[2 * s + p, :, 0:128] = landed[s, :, 128 * p : 128 * (p + 1)]
            out[2 * s + p, :, 128:160] = landed[s, :, 256 + 32 * p : 256 + 32 * (p + 1)]

    for copy in copies:
        copy.wait_send()

    @pl.loop(0, 16)
    def _(t):
        @pl.when(16 * core + t != me)
        def _():
            src = flipped.at[pl.ds(pl.multiple_of(40 * t, 8), 40)]
            pltpu.make_async_remote_copy(
                src_ref=src, dst_ref=landed.at[chip], send_sem=last_send.at[t], recv_sem=last_recv.at[chip],
                device_id=(16 * core + t, z), device_id_type=MESH,
            ).wait_send()


def local(depth, integrals, coefficients, block_nu, block_count):
    mu_blocks, slots, _, area = integrals.shape
    rows, orbitals = coefficients.shape
    width = orbitals // 2
    blocks = 96
    bf16, f32 = jnp.bfloat16, jnp.float32
    messages = 136
    return pl.pallas_call(
        functools.partial(kernel, depth),
        out_shape=jax.ShapeDtypeStruct((32, 40, 160), f32),
        in_specs=[
            pl.BlockSpec(memory_space=pl.ANY),
            pl.BlockSpec(memory_space=pl.ANY),
            pl.BlockSpec(memory_space=pltpu.SMEM),
            pl.BlockSpec(memory_space=pltpu.SMEM),
        ],
        out_specs=pl.BlockSpec(memory_space=pltpu.VMEM),
        scratch_shapes=[
            pltpu.VMEM((mu_blocks, slots, area), bf16),
            pltpu.VMEM((blocks, BLK, width), bf16),
            pltpu.VMEM((mu_blocks, 2 * BLK, slots * BLK), bf16),
            pltpu.VMEM((mu_blocks, BLK, width), bf16),
            pltpu.VMEM((8, 160, mu_blocks * BLK), bf16),
            pltpu.VMEM((2, mu_blocks * BLK, width), bf16),
            pltpu.VMEM((2, 7, 160, width), bf16),
            pltpu.VMEM((2, 7, 160, width), bf16),
            pltpu.VMEM((384, width), f32),
            pltpu.VMEM((width, 384), f32),
            pltpu.VMEM((16, 40, 384), f32),
            pltpu.SemaphoreType.DMA((2,)),
            pltpu.SemaphoreType.DMA((messages,)),
            pltpu.SemaphoreType.DMA((messages,)),
            pltpu.SemaphoreType.DMA((16,)),
            pltpu.SemaphoreType.DMA((16,)),
        ],
        compiler_params=pltpu.CompilerParams(
            collective_id=0, has_side_effects=True, vmem_limit_bytes=52 * 1024 * 1024
        ),
        cost_estimate=pl.CostEstimate(flops=6_000_000_000, bytes_accessed=4_000_000, transcendentals=0),
    )(
        integrals.reshape(mu_blocks, slots, area),
        coefficients.reshape(rows // BLK, BLK, orbitals),
        block_nu,
        block_count,
    )


def solution(mesh):
    placed = (P("basis", None, "aux", None), P("aux", None), P("basis", None), P("basis"))
    return jax.shard_map(
        functools.partial(local, mesh.shape["basis"]),
        mesh=mesh,
        in_specs=placed,
        out_specs=P(None, "aux", "basis"),
        check_vma=False,
    )
```

```python
import functools

import jax
import jax.numpy as jnp
from jax import lax
from jax.experimental import pallas as pl
from jax.experimental.pallas import tpu as pltpu
from jax.sharding import PartitionSpec as P

BLK = 64
SIDE = 4
MESH = pl.DeviceIdType.MESH
PARTS = ((0, 96), (96, 64))


def relayout(raw, count, target, m, first_row):
    slots, area = raw.shape[1:]
    values = raw[m].astype(jnp.float32)
    slot_ids = lax.broadcasted_iota(jnp.int32, (slots, area), 0)
    values = jnp.where(slot_ids < count, values, 0.0)
    pairs = area // (2 * BLK)
    by_pair = jnp.stack([values[:, 2 * BLK * a : 2 * BLK * (a + 1)] for a in range(pairs)], axis=0)
    by_slot = jnp.swapaxes(by_pair, 0, 1)
    low = lax.broadcasted_iota(jnp.int32, (pairs, 2 * BLK), 1) < BLK
    for k in range(0, slots, 2):
        one, two = by_slot[k], by_slot[k + 1]
        even = jnp.where(low, one, pltpu.roll(two, BLK, 1))
        odd = jnp.where(low, pltpu.roll(one, BLK, 1), two)
        columns = slice(BLK * k, BLK * (k + 2))
        target[m, pl.ds(first_row, pairs), columns] = even.astype(jnp.bfloat16)
        target[m, pl.ds(first_row + pairs, pairs), columns] = odd.astype(jnp.bfloat16)


def turned(blocks, first_block):
    new = lax.broadcasted_iota(jnp.int32, (BLK, BLK), 1)
    old = lax.broadcasted_iota(jnp.int32, (BLK, BLK), 0)
    source = jnp.where(new < BLK // 2, 2 * new, 2 * new - BLK + 1)
    order = (old == source).astype(jnp.bfloat16)
    columns = [
        lax.dot_general(
            blocks[first_block + m], order, (((0,), (0,)), ((), ())), preferred_element_type=jnp.float32
        )
        for m in range(12)
    ]
    return jnp.concatenate(columns, axis=1).astype(jnp.bfloat16)


def kernel(
    depth, integrals, shard, nu_in, count_in, out,
    raw, block_nu, block_count, coef, mats, other, turned_rows, half, outgoing, incoming, finals, flips, landed,
    local_sems, send_sems, recv_sems, last_send, last_recv,
):
    me = lax.axis_index("aux")
    z = lax.axis_index("basis")
    core = lax.rem(me, 2)
    chip = lax.div(me, 2)
    x = lax.div(chip, SIDE)
    y = lax.rem(chip, SIDE)
    width = coef.shape[2]
    mu_blocks = raw.shape[0]
    group = 6

    def device(dx, dy, dz=0, core_at=core):
        at_x = lax.rem(x + dx + SIDE, SIDE)
        at_y = lax.rem(y + dy + SIDE, SIDE)
        return ((at_x * SIDE + at_y) * 2 + core_at, lax.rem(z + dz + depth, depth))

    partner = device(0, 0, 0, 1 - core)

    fetches = [
        pltpu.make_async_copy(src, dst, local_sems.at[k])
        for k, (src, dst) in enumerate(((integrals, raw), (nu_in, block_nu), (count_in, block_count)))
    ]
    mine = coef.at[pl.ds(group * chip + 3 * core, 3)]
    keep = pltpu.make_async_copy(
        shard.at[:, :, pl.ds(pl.multiple_of(width * core, 128), width)], mine, local_sems.at[3]
    )
    keep.start()
    for fetch in fetches:
        fetch.start()

    barrier = pltpu.get_barrier_semaphore()
    for friend in (
        device(1, 0), device(-1, 0), device(0, 1), device(0, -1), device(0, 0, 1), device(0, 0, -1), partner,
    ):
        pl.semaphore_signal(barrier, inc=1, device_id=friend, device_id_type=MESH)
    sender_core = lax.div(me, 16)

    @pl.loop(0, 16)
    def _(s):
        sender = 2 * s + sender_core

        @pl.when(sender != me)
        def _():
            pl.semaphore_signal(barrier, inc=1, device_id=(sender, z), device_id_type=MESH)

    pl.semaphore_wait(barrier, jnp.where(sender_core == core, 7 + 15, 7 + 16))

    copies = []

    def send(src, dst, target):
        k = len(copies)
        copy = pltpu.make_async_remote_copy(
            src_ref=src, dst_ref=dst, send_sem=send_sems.at[k], recv_sem=recv_sems.at[k],
            device_id=target, device_id_type=MESH,
        )
        copy.start()
        copies.append(copy)
        return copy

    swap = send(shard.at[:, :, pl.ds(pl.multiple_of(width * (1 - core), 128), width)], mine, partner)
    keep.wait()
    swap.wait_recv()

    parity = lax.rem(z, 2)

    class Stream:
        def __init__(self, offset, along_x, up):
            self.offset, self.along_x, self.up = offset, along_x, up
            self.plus, self.minus, self.far = {}, {}, {}

        def device(self, df, dg):
            return device(df, dg) if self.along_x else device(dg, df)

        def block(self, df, dg):
            dx, dy = (df, dg) if self.along_x else (dg, df)
            at_x = lax.rem(x + dx + SIDE, SIDE)
            at_y = lax.rem(y + dy + SIDE, SIDE)
            return coef.at[group * (at_x * SIDE + at_y) + self.offset]

        def first(self):
            block = self.block(0, 0)
            self.first_plus = send(block, block, self.device(1, 0))
            self.first_minus = send(block, block, self.device(-1, 0))

        def first_on(self):
            self.first_plus.wait_recv()
            low = self.block(-1, 0).at[pl.ds(0, BLK // 2)]
            self.far_low = send(low, low, self.device(1, 0))
            self.first_minus.wait_recv()
            high = self.block(1, 0).at[pl.ds(BLK // 2, BLK // 2)]
            self.far_high = send(high, high, self.device(-1, 0))

        def first_end(self):
            self.far_low.wait_recv()
            self.far_high.wait_recv()

        def second(self, df):
            block = self.block(df, 0)
            self.plus[df] = send(block, block, self.device(0, 1))
            self.minus[df] = send(block, block, self.device(0, -1))

        def second_on(self, df):
            self.plus[df].wait_recv()
            low = self.block(df, -1).at[pl.ds(0, BLK // 2)]
            low_copy = send(low, low, self.device(0, 1))
            self.minus[df].wait_recv()
            high = self.block(df, 1).at[pl.ds(BLK // 2, BLK // 2)]
            self.far[df] = (low_copy, send(high, high, self.device(0, -1)))

        def second_end(self, df):
            for copy in self.far[df]:
                copy.wait_recv()

        def beside(self, df, dg):
            if self.up:
                block = self.block(df, dg)
                from_beside.append(send(block, block, device(0, 0, self.up)))

    from_beside = []
    streams = [
        Stream(2 + 2 * parity, True, 1),
        Stream(3 + 2 * parity, False, -1),
        Stream(0, True, 0),
        Stream(1, False, 0),
    ]
    fetched = [False]

    def bring(begin, end):
        if not fetched[0]:
            for fetch in fetches:
                fetch.wait()
            fetched[0] = True

        @pl.loop(begin, end)
        def _(m):
            relayout(raw, block_count[m], mats, m, pl.multiple_of(BLK * core, BLK))

        part = mats.at[pl.ds(begin, end - begin), pl.ds(pl.multiple_of(BLK * core, BLK), BLK)]
        return send(part, part, partner)

    beside_streams, plain_streams = streams[:2], streams[2:]
    for stream in streams:
        stream.first()
    for stream in beside_streams:
        stream.second(0)
    mats_in = [bring(0, 4)]
    for stream in beside_streams:
        stream.first_on()
        stream.beside(-1, 0)
        stream.beside(1, 0)
    for df in (-1, 1):
        for stream in beside_streams:
            stream.second(df)
    for stream in plain_streams:
        stream.first_on()
    for stream in beside_streams:
        stream.first_end()
        stream.second(2)
        stream.beside(2, 0)
    for stream in beside_streams:
        stream.second_on(0)
        stream.beside(0, -1)
        stream.beside(0, 1)
    for df in (0, -1, 1):
        for stream in plain_streams:
            stream.second(df)
    for stream in plain_streams:
        stream.first_end()
        stream.second(2)
    mats_in.append(bring(4, 8))
    before = 0
    for df in (-1, 1, 2):
        for stream in beside_streams:
            stream.second_on(df)
            stream.beside(df, -1)
            stream.beside(df, 1)
            stream.second_end(before)
            stream.beside(before, 2)
        before = df
    for stream in plain_streams:
        stream.second_on(0)
    for stream in beside_streams:
        stream.second_end(2)
        stream.beside(2, 2)
    mats_in.append(bring(8, 12))
    for df in (-1, 1, 2):
        for stream in plain_streams:
            stream.second_on(df)
    for df in (0, -1, 1, 2):
        for stream in plain_streams:
            stream.second_end(df)
    for copy in from_beside:
        copy.wait_recv()

    own_first = mu_blocks * z
    other_in = send(coef.at[pl.ds(own_first, mu_blocks)], other, partner)
    per_core = 4

    def place(rows, at_core):
        for q in range(per_core):
            turned_rows[per_core * at_core + q] = rows[160 * q : 160 * (q + 1)]

    place(turned(coef, own_first), core)
    for copy in mats_in:
        copy.wait_recv()

    @pl.loop(0, mu_blocks)
    def _(m):
        picked = jnp.concatenate([coef[block_nu[m, k]] for k in range(raw.shape[1])], axis=0)
        product = jnp.dot(mats[m], picked, preferred_element_type=jnp.float32)
        rows = pl.ds(pl.multiple_of(m * BLK, BLK), BLK)
        half[0, rows, :] = product[:BLK].astype(jnp.bfloat16)
        half[1, rows, :] = product[BLK:].astype(jnp.bfloat16)

    other_in.wait_recv()
    place(turned(other, 0), 1 - core)

    def partial_sum(part, target, p):
        first, count = PARTS[part]
        return jnp.dot(
            turned_rows[target, first : first + count, :], half[p], preferred_element_type=jnp.float32
        )

    rings = [[[], []] for _ in PARTS]

    def ring_step(part, k):
        distance = 4 - (k + 1) // 2
        for way in range(2):
            ring = rings[part][way]
            p = k % 2 if way == 0 else 1 - k % 2
            step = distance if way == 0 else -distance
            value = partial_sum(part, lax.rem(z + step + depth, depth), p)
            if k >= 2:
                ring[k - 2].wait_recv()
                value = value + incoming[part][way, k - 2].astype(jnp.float32)
            outgoing[part][way, k] = value.astype(jnp.bfloat16)
            ring.append(
                send(
                    outgoing[part].at[way, k], incoming[part].at[way, k], device(0, 0, 1 if way == 0 else -1)
                )
            )

    def ring_end(part):
        count = PARTS[part][1]
        own = [partial_sum(part, z, p) for p in range(2)]
        final = finals[part]
        for way in range(2):
            for k in (5, 6):
                rings[part][way][k].wait_recv()
        for p in range(2):
            up, down = (6, 5) if p == 0 else (5, 6)
            value = own[p] + incoming[part][0, up].astype(jnp.float32)
            final[count * p : count * (p + 1), :] = value + incoming[part][1, down].astype(jnp.float32)
        if 2 * count < final.shape[0]:
            final[2 * count :, :] = jnp.zeros((final.shape[0] - 2 * count, width), jnp.float32)
        flips[part][...] = jnp.transpose(final[...], (1, 0))

    def last_copy(part, t):
        src = flips[part].at[pl.ds(pl.multiple_of(40 * t, 8), 40)]
        dst = landed[part].at[chip]
        owner = 16 * core + t

        def remote():
            return pltpu.make_async_remote_copy(
                src_ref=src, dst_ref=dst, send_sem=last_send.at[part, t], recv_sem=last_recv.at[part, chip],
                device_id=(owner, z), device_id_type=MESH,
            )

        return owner, remote, lambda: pltpu.make_async_copy(src, dst, last_recv.at[part, chip])

    def give(part):
        @pl.loop(0, 16)
        def _(i):
            owner, remote, here = last_copy(part, lax.rem(chip + i, 16))

            @pl.when(owner == me)
            def _():
                here().start()

            @pl.when(owner != me)
            def _():
                remote().start()

    def take(part):
        first, count = PARTS[part]
        for s in range(16):
            block = landed[part].at[s]
            pltpu.make_async_copy(block, block, last_recv.at[part, s]).wait()
            for p in range(2):
                out[2 * s + p, :, first : first + count] = landed[part][s, :, count * p : count * (p + 1)]

    for k in range(5):
        ring_step(0, k)
    ring_step(1, 0)
    ring_step(0, 5)
    ring_step(1, 1)
    ring_step(0, 6)
    ring_step(1, 2)
    ring_end(0)
    give(0)
    for k in range(3, 7):
        ring_step(1, k)
    take(0)
    ring_end(1)
    give(1)
    take(1)

    for copy in copies:
        copy.wait_send()

    @pl.loop(0, 16)
    def _(t):
        for part in range(len(PARTS)):
            owner, remote, _ = last_copy(part, t)

            @pl.when(owner != me)
            def _():
                remote().wait_send()


def local(depth, integrals, coefficients, block_nu, block_count):
    mu_blocks, slots, _, area = integrals.shape
    rows, orbitals = coefficients.shape
    width = orbitals // 2
    blocks = 96
    bf16, f32 = jnp.bfloat16, jnp.float32
    messages = 160
    return pl.pallas_call(
        functools.partial(kernel, depth),
        out_shape=jax.ShapeDtypeStruct((32, 40, 160), f32),
        in_specs=[
            pl.BlockSpec(memory_space=pl.ANY),
            pl.BlockSpec(memory_space=pl.ANY),
            pl.BlockSpec(memory_space=pl.ANY),
            pl.BlockSpec(memory_space=pl.ANY),
        ],
        out_specs=pl.BlockSpec(memory_space=pltpu.VMEM),
        scratch_shapes=[
            pltpu.VMEM((mu_blocks, slots, area), bf16),
            pltpu.SMEM((mu_blocks, slots), jnp.int32),
            pltpu.SMEM((mu_blocks,), jnp.int32),
            pltpu.VMEM((blocks, BLK, width), bf16),
            pltpu.VMEM((mu_blocks, 2 * BLK, slots * BLK), bf16),
            pltpu.VMEM((mu_blocks, BLK, width), bf16),
            pltpu.VMEM((8, 160, mu_blocks * BLK), bf16),
            pltpu.VMEM((2, mu_blocks * BLK, width), bf16),
            [pltpu.VMEM((2, 7, count, width), bf16) for _, count in PARTS],
            [pltpu.VMEM((2, 7, count, width), bf16) for _, count in PARTS],
            [pltpu.VMEM((lanes, width), f32) for lanes in (256, 128)],
            [pltpu.VMEM((width, lanes), f32) for lanes in (256, 128)],
            [pltpu.VMEM((16, 40, lanes), f32) for lanes in (256, 128)],
            pltpu.SemaphoreType.DMA((4,)),
            pltpu.SemaphoreType.DMA((messages,)),
            pltpu.SemaphoreType.DMA((messages,)),
            pltpu.SemaphoreType.DMA((len(PARTS), 16)),
            pltpu.SemaphoreType.DMA((len(PARTS), 16)),
        ],
        compiler_params=pltpu.CompilerParams(
            collective_id=0, has_side_effects=True, vmem_limit_bytes=60 * 1024 * 1024
        ),
        cost_estimate=pl.CostEstimate(flops=6_000_000_000, bytes_accessed=4_000_000, transcendentals=0),
    )(
        integrals.reshape(mu_blocks, slots, area),
        coefficients.reshape(rows // BLK, BLK, orbitals),
        block_nu,
        block_count,
    )


def solution(mesh):
    placed = (P("basis", None, "aux", None), P("aux", None), P("basis", None), P("basis"))
    return jax.shard_map(
        functools.partial(local, mesh.shape["basis"]),
        mesh=mesh,
        in_specs=placed,
        out_specs=P(None, "aux", "basis"),
        check_vma=False,
    )
```

```python
import functools

import jax
import jax.numpy as jnp
from jax import lax
from jax.experimental import pallas as pl
from jax.experimental.pallas import tpu as pltpu
from jax.sharding import PartitionSpec as P

BLK = 64
SIDE = 4
MESH = pl.DeviceIdType.MESH
PARTS = ((0, 96), (96, 64))


def relayout(raw, count, target, m, first_row):
    slots, area = raw.shape[1:]
    values = raw[m].astype(jnp.float32)
    slot_ids = lax.broadcasted_iota(jnp.int32, (slots, area), 0)
    values = jnp.where(slot_ids < count, values, 0.0)
    pairs = area // (2 * BLK)
    by_pair = jnp.stack([values[:, 2 * BLK * a : 2 * BLK * (a + 1)] for a in range(pairs)], axis=0)
    by_slot = jnp.swapaxes(by_pair, 0, 1)
    low = lax.broadcasted_iota(jnp.int32, (pairs, 2 * BLK), 1) < BLK
    for k in range(0, slots, 2):
        one, two = by_slot[k], by_slot[k + 1]
        even = jnp.where(low, one, pltpu.roll(two, BLK, 1))
        odd = jnp.where(low, pltpu.roll(one, BLK, 1), two)
        columns = slice(BLK * k, BLK * (k + 2))
        target[m, pl.ds(first_row, pairs), columns] = even.astype(jnp.bfloat16)
        target[m, pl.ds(first_row + pairs, pairs), columns] = odd.astype(jnp.bfloat16)


def turned(blocks, first_block):
    new = lax.broadcasted_iota(jnp.int32, (BLK, BLK), 1)
    old = lax.broadcasted_iota(jnp.int32, (BLK, BLK), 0)
    source = jnp.where(new < BLK // 2, 2 * new, 2 * new - BLK + 1)
    order = (old == source).astype(jnp.bfloat16)
    columns = [
        lax.dot_general(
            blocks[first_block + m], order, (((0,), (0,)), ((), ())), preferred_element_type=jnp.float32
        )
        for m in range(12)
    ]
    return jnp.concatenate(columns, axis=1).astype(jnp.bfloat16)


def kernel(
    depth, integrals, shard, nu_in, count_in, out,
    raw, block_nu, block_count, coef, mats, other, turned_rows, half, outgoing, incoming, finals, flips, landed,
    local_sems, send_sems, recv_sems, last_send, last_recv,
):
    me = lax.axis_index("aux")
    z = lax.axis_index("basis")
    core = lax.rem(me, 2)
    chip = lax.div(me, 2)
    x = lax.div(chip, SIDE)
    y = lax.rem(chip, SIDE)
    width = coef.shape[2]
    mu_blocks = raw.shape[0]
    group = 6

    def device(dx, dy, dz=0, core_at=core):
        at_x = lax.rem(x + dx + SIDE, SIDE)
        at_y = lax.rem(y + dy + SIDE, SIDE)
        return ((at_x * SIDE + at_y) * 2 + core_at, lax.rem(z + dz + depth, depth))

    partner = device(0, 0, 0, 1 - core)

    fetches = [
        pltpu.make_async_copy(src, dst, local_sems.at[k])
        for k, (src, dst) in enumerate(((integrals, raw), (nu_in, block_nu), (count_in, block_count)))
    ]
    mine = coef.at[pl.ds(group * chip + 3 * core, 3)]
    keep = pltpu.make_async_copy(
        shard.at[:, :, pl.ds(pl.multiple_of(width * core, 128), width)], mine, local_sems.at[3]
    )
    keep.start()
    for fetch in fetches:
        fetch.start()

    barrier = pltpu.get_barrier_semaphore()
    for friend in (
        device(1, 0), device(-1, 0), device(0, 1), device(0, -1), device(0, 0, 1), device(0, 0, -1), partner,
    ):
        pl.semaphore_signal(barrier, inc=1, device_id=friend, device_id_type=MESH)

    own_rows = pl.ds(pl.multiple_of(BLK * core, BLK), BLK)
    for fetch in fetches:
        fetch.wait()

    @pl.loop(0, mu_blocks)
    def _(m):
        relayout(raw, block_count[m], mats, m, pl.multiple_of(BLK * core, BLK))

    pl.semaphore_wait(barrier, 7)

    copies = []

    def send(src, dst, target):
        k = len(copies)
        copy = pltpu.make_async_remote_copy(
            src_ref=src, dst_ref=dst, send_sem=send_sems.at[k], recv_sem=recv_sems.at[k],
            device_id=target, device_id_type=MESH,
        )
        copy.start()
        copies.append(copy)
        return copy

    swap = send(shard.at[:, :, pl.ds(pl.multiple_of(width * (1 - core), 128), width)], mine, partner)
    keep.wait()
    swap.wait_recv()

    parity = lax.rem(z, 2)

    class Stream:
        def __init__(self, offset, along_x, up):
            self.offset, self.along_x, self.up = offset, along_x, up
            self.plus, self.minus, self.far = {}, {}, {}

        def device(self, df, dg):
            return device(df, dg) if self.along_x else device(dg, df)

        def block(self, df, dg):
            dx, dy = (df, dg) if self.along_x else (dg, df)
            at_x = lax.rem(x + dx + SIDE, SIDE)
            at_y = lax.rem(y + dy + SIDE, SIDE)
            return coef.at[group * (at_x * SIDE + at_y) + self.offset]

        def first(self):
            block = self.block(0, 0)
            self.first_plus = send(block, block, self.device(1, 0))
            self.first_minus = send(block, block, self.device(-1, 0))

        def first_on(self):
            self.first_plus.wait_recv()
            low = self.block(-1, 0).at[pl.ds(0, BLK // 2)]
            self.far_low = send(low, low, self.device(1, 0))
            self.first_minus.wait_recv()
            high = self.block(1, 0).at[pl.ds(BLK // 2, BLK // 2)]
            self.far_high = send(high, high, self.device(-1, 0))

        def first_end(self):
            self.far_low.wait_recv()
            self.far_high.wait_recv()

        def second(self, df):
            block = self.block(df, 0)
            self.plus[df] = send(block, block, self.device(0, 1))
            self.minus[df] = send(block, block, self.device(0, -1))

        def second_on(self, df):
            self.plus[df].wait_recv()
            low = self.block(df, -1).at[pl.ds(0, BLK // 2)]
            low_copy = send(low, low, self.device(0, 1))
            self.minus[df].wait_recv()
            high = self.block(df, 1).at[pl.ds(BLK // 2, BLK // 2)]
            self.far[df] = (low_copy, send(high, high, self.device(0, -1)))

        def second_end(self, df):
            for copy in self.far[df]:
                copy.wait_recv()

        def beside(self, df, dg):
            if self.up:
                block = self.block(df, dg)
                from_beside.append(send(block, block, device(0, 0, self.up)))

    from_beside = []
    streams = [
        Stream(2 + 2 * parity, True, 1),
        Stream(3 + 2 * parity, False, -1),
        Stream(0, True, 0),
        Stream(1, False, 0),
    ]
    def bring(begin, end):
        share = mats.at[pl.ds(begin, end - begin), own_rows]
        return send(share, share, partner)

    beside_streams, plain_streams = streams[:2], streams[2:]
    for stream in beside_streams:
        stream.first()
    for stream in beside_streams:
        stream.second(0)
    for stream in beside_streams:
        stream.first_on()
        stream.beside(-1, 0)
        stream.beside(1, 0)
    for stream in beside_streams:
        stream.second(-1)
    for stream in beside_streams:
        stream.second(1)
    for stream in plain_streams:
        stream.first()
    mats_in = [bring(0, mu_blocks)]
    for stream in beside_streams:
        stream.first_end()
        stream.beside(2, 0)
    for stream in beside_streams:
        stream.second(2)
    for stream in beside_streams:
        stream.second_on(0)
        stream.beside(0, -1)
        stream.beside(0, 1)
    for stream in plain_streams:
        stream.second(0)
    for stream in plain_streams:
        stream.first_on()
        stream.beside(-1, 0)
        stream.beside(1, 0)
    for stream in plain_streams:
        stream.second(-1)
    for stream in plain_streams:
        stream.second(1)
    for stream in beside_streams:
        stream.second_on(-1)
        stream.beside(-1, -1)
        stream.beside(-1, 1)
    for stream in beside_streams:
        stream.second_end(0)
        stream.beside(0, 2)
    for stream in plain_streams:
        stream.first_end()
        stream.beside(2, 0)
    for stream in plain_streams:
        stream.second(2)
    for stream in beside_streams:
        stream.second_on(1)
        stream.beside(1, -1)
        stream.beside(1, 1)
    for stream in beside_streams:
        stream.second_end(-1)
        stream.beside(-1, 2)
    for stream in plain_streams:
        stream.second_on(0)
        stream.beside(0, -1)
        stream.beside(0, 1)
    for stream in beside_streams:
        stream.second_on(2)
        stream.beside(2, -1)
        stream.beside(2, 1)
    for stream in beside_streams:
        stream.second_end(1)
        stream.beside(1, 2)
    for stream in plain_streams:
        stream.second_on(-1)
        stream.beside(-1, -1)
        stream.beside(-1, 1)
    for stream in beside_streams:
        stream.second_end(2)
        stream.beside(2, 2)
    for stream in plain_streams:
        stream.second_on(1)
        stream.beside(1, -1)
        stream.beside(1, 1)
    for stream in plain_streams:
        stream.second_on(2)
        stream.beside(2, -1)
        stream.beside(2, 1)
    for stream in plain_streams:
        stream.second_end(0)
        stream.beside(0, 2)
    for stream in plain_streams:
        stream.second_end(-1)
        stream.beside(-1, 2)
    for stream in plain_streams:
        stream.second_end(1)
        stream.beside(1, 2)
    for stream in plain_streams:
        stream.second_end(2)
        stream.beside(2, 2)
    for copy in from_beside:
        copy.wait_recv()

    own_first = mu_blocks * z
    other_in = send(coef.at[pl.ds(own_first, mu_blocks)], other, partner)
    per_core = 4

    def place(rows, at_core):
        for q in range(per_core):
            turned_rows[per_core * at_core + q] = rows[160 * q : 160 * (q + 1)]

    place(turned(coef, own_first), core)
    for copy in mats_in:
        copy.wait_recv()

    @pl.loop(0, mu_blocks)
    def _(m):
        picked = jnp.concatenate([coef[block_nu[m, k]] for k in range(raw.shape[1])], axis=0)
        product = jnp.dot(mats[m], picked, preferred_element_type=jnp.float32)
        rows = pl.ds(pl.multiple_of(m * BLK, BLK), BLK)
        half[0, rows, :] = product[:BLK].astype(jnp.bfloat16)
        half[1, rows, :] = product[BLK:].astype(jnp.bfloat16)

    other_in.wait_recv()
    place(turned(other, 0), 1 - core)

    def partial_sum(part, target, p):
        first, count = PARTS[part]
        return jnp.dot(
            turned_rows[target, first : first + count, :], half[p], preferred_element_type=jnp.float32
        )

    rings = [[[], []] for _ in PARTS]

    def ring_step(part, k):
        distance = 4 - (k + 1) // 2
        for way in range(2):
            ring = rings[part][way]
            p = k % 2 if way == 0 else 1 - k % 2
            step = distance if way == 0 else -distance
            value = partial_sum(part, lax.rem(z + step + depth, depth), p)
            if k >= 2:
                ring[k - 2].wait_recv()
                value = value + incoming[part][way, k - 2].astype(jnp.float32)
            outgoing[part][way, k] = value.astype(jnp.bfloat16)
            ring.append(
                send(
                    outgoing[part].at[way, k], incoming[part].at[way, k], device(0, 0, 1 if way == 0 else -1)
                )
            )

    def ring_end(part):
        count = PARTS[part][1]
        own = [partial_sum(part, z, p) for p in range(2)]
        final = finals[part]
        for way in range(2):
            for k in (5, 6):
                rings[part][way][k].wait_recv()
        for p in range(2):
            up, down = (6, 5) if p == 0 else (5, 6)
            value = own[p] + incoming[part][0, up].astype(jnp.float32)
            final[count * p : count * (p + 1), :] = value + incoming[part][1, down].astype(jnp.float32)
        if 2 * count < final.shape[0]:
            final[2 * count :, :] = jnp.zeros((final.shape[0] - 2 * count, width), jnp.float32)
        flips[part][...] = jnp.transpose(final[...], (1, 0))

    def last_copy(part, t):
        src = flips[part].at[pl.ds(pl.multiple_of(40 * t, 8), 40)]
        dst = landed[part].at[chip]
        owner = 16 * core + t

        def remote():
            return pltpu.make_async_remote_copy(
                src_ref=src, dst_ref=dst, send_sem=last_send.at[part, t], recv_sem=last_recv.at[part, chip],
                device_id=(owner, z), device_id_type=MESH,
            )

        return owner, remote, lambda: pltpu.make_async_copy(src, dst, last_recv.at[part, chip])

    def give(part):
        @pl.loop(0, 16)
        def _(i):
            owner, remote, here = last_copy(part, lax.rem(chip + i, 16))

            @pl.when(owner == me)
            def _():
                here().start()

            @pl.when(owner != me)
            def _():
                remote().start()

    def take(part):
        first, count = PARTS[part]
        for s in range(16):
            block = landed[part].at[s]
            pltpu.make_async_copy(block, block, last_recv.at[part, s]).wait()
            for p in range(2):
                out[2 * s + p, :, first : first + count] = landed[part][s, :, count * p : count * (p + 1)]

    for part, k in (
        (0, 0), (0, 1), (0, 2), (1, 0), (0, 3), (1, 1), (0, 4), (1, 2), (0, 5), (1, 3), (0, 6), (1, 4), (1, 5),
    ):
        ring_step(part, k)
    ring_end(0)
    give(0)
    ring_step(1, 6)
    take(0)
    ring_end(1)
    give(1)
    take(1)

    for copy in copies:
        copy.wait_send()

    @pl.loop(0, 16)
    def _(t):
        for part in range(len(PARTS)):
            owner, remote, _ = last_copy(part, t)

            @pl.when(owner != me)
            def _():
                remote().wait_send()


def local(depth, integrals, coefficients, block_nu, block_count):
    mu_blocks, slots, _, area = integrals.shape
    rows, orbitals = coefficients.shape
    width = orbitals // 2
    blocks = 96
    bf16, f32 = jnp.bfloat16, jnp.float32
    messages = 160
    return pl.pallas_call(
        functools.partial(kernel, depth),
        out_shape=jax.ShapeDtypeStruct((32, 40, 160), f32),
        in_specs=[
            pl.BlockSpec(memory_space=pl.ANY),
            pl.BlockSpec(memory_space=pl.ANY),
            pl.BlockSpec(memory_space=pl.ANY),
            pl.BlockSpec(memory_space=pl.ANY),
        ],
        out_specs=pl.BlockSpec(memory_space=pltpu.VMEM),
        scratch_shapes=[
            pltpu.VMEM((mu_blocks, slots, area), bf16),
            pltpu.SMEM((mu_blocks, slots), jnp.int32),
            pltpu.SMEM((mu_blocks,), jnp.int32),
            pltpu.VMEM((blocks, BLK, width), bf16),
            pltpu.VMEM((mu_blocks, 2 * BLK, slots * BLK), bf16),
            pltpu.VMEM((mu_blocks, BLK, width), bf16),
            pltpu.VMEM((8, 160, mu_blocks * BLK), bf16),
            pltpu.VMEM((2, mu_blocks * BLK, width), bf16),
            [pltpu.VMEM((2, 7, count, width), bf16) for _, count in PARTS],
            [pltpu.VMEM((2, 7, count, width), bf16) for _, count in PARTS],
            [pltpu.VMEM((lanes, width), f32) for lanes in (256, 128)],
            [pltpu.VMEM((width, lanes), f32) for lanes in (256, 128)],
            [pltpu.VMEM((16, 40, lanes), f32) for lanes in (256, 128)],
            pltpu.SemaphoreType.DMA((4,)),
            pltpu.SemaphoreType.DMA((messages,)),
            pltpu.SemaphoreType.DMA((messages,)),
            pltpu.SemaphoreType.DMA((len(PARTS), 16)),
            pltpu.SemaphoreType.DMA((len(PARTS), 16)),
        ],
        compiler_params=pltpu.CompilerParams(
            collective_id=0, has_side_effects=True, vmem_limit_bytes=60 * 1024 * 1024
        ),
        cost_estimate=pl.CostEstimate(flops=6_000_000_000, bytes_accessed=4_000_000, transcendentals=0),
    )(
        integrals.reshape(mu_blocks, slots, area),
        coefficients.reshape(rows // BLK, BLK, orbitals),
        block_nu,
        block_count,
    )


def solution(mesh):
    placed = (P("basis", None, "aux", None), P("aux", None), P("basis", None), P("basis"))
    return jax.shard_map(
        functools.partial(local, mesh.shape["basis"]),
        mesh=mesh,
        in_specs=placed,
        out_specs=P(None, "aux", "basis"),
        check_vma=False,
    )
```

```python
import functools

import jax
import jax.numpy as jnp
from jax import lax
from jax.experimental import pallas as pl
from jax.experimental.pallas import tpu as pltpu
from jax.sharding import PartitionSpec as P

BLK = 64
SIDE = 4
MESH = pl.DeviceIdType.MESH
PARTS = ((0, 96), (96, 64))


def relayout(raw, count, target, m, first_row):
    slots, area = raw.shape[1:]
    values = raw[m].astype(jnp.float32)
    slot_ids = lax.broadcasted_iota(jnp.int32, (slots, area), 0)
    values = jnp.where(slot_ids < count, values, 0.0)
    pairs = area // (2 * BLK)
    by_pair = jnp.stack([values[:, 2 * BLK * a : 2 * BLK * (a + 1)] for a in range(pairs)], axis=0)
    by_slot = jnp.swapaxes(by_pair, 0, 1)
    low = lax.broadcasted_iota(jnp.int32, (pairs, 2 * BLK), 1) < BLK
    for k in range(0, slots, 2):
        one, two = by_slot[k], by_slot[k + 1]
        even = jnp.where(low, one, pltpu.roll(two, BLK, 1))
        odd = jnp.where(low, pltpu.roll(one, BLK, 1), two)
        columns = slice(BLK * k, BLK * (k + 2))
        target[m, pl.ds(first_row, pairs), columns] = even.astype(jnp.bfloat16)
        target[m, pl.ds(first_row + pairs, pairs), columns] = odd.astype(jnp.bfloat16)


def turned(blocks, first_block):
    new = lax.broadcasted_iota(jnp.int32, (BLK, BLK), 1)
    old = lax.broadcasted_iota(jnp.int32, (BLK, BLK), 0)
    source = jnp.where(new < BLK // 2, 2 * new, 2 * new - BLK + 1)
    order = (old == source).astype(jnp.bfloat16)
    columns = [
        lax.dot_general(
            blocks[first_block + m], order, (((0,), (0,)), ((), ())), preferred_element_type=jnp.float32
        )
        for m in range(12)
    ]
    return jnp.concatenate(columns, axis=1).astype(jnp.bfloat16)


def kernel(
    depth, integrals, shard, nu_in, count_in, result,
    out, raw, block_nu, block_count, coef, mats, other, turned_rows, half, outgoing, incoming, finals, flips, landed,
    local_sems, out_sems, send_sems, recv_sems, last_send, last_recv,
):
    me = lax.axis_index("aux")
    z = lax.axis_index("basis")
    core = lax.rem(me, 2)
    chip = lax.div(me, 2)
    x = lax.div(chip, SIDE)
    y = lax.rem(chip, SIDE)
    width = coef.shape[2]
    mu_blocks = raw.shape[0]
    group = 6

    def device(dx, dy, dz=0, core_at=core):
        at_x = lax.rem(x + dx + SIDE, SIDE)
        at_y = lax.rem(y + dy + SIDE, SIDE)
        return ((at_x * SIDE + at_y) * 2 + core_at, lax.rem(z + dz + depth, depth))

    partner = device(0, 0, 0, 1 - core)

    barrier = pltpu.get_barrier_semaphore()
    for friend in (
        device(1, 0), device(-1, 0), device(0, 1), device(0, -1), device(0, 0, 1), device(0, 0, -1), partner,
    ):
        pl.semaphore_signal(barrier, inc=1, device_id=friend, device_id_type=MESH)

    fetches = [
        pltpu.make_async_copy(src, dst, local_sems.at[k])
        for k, (src, dst) in enumerate(((integrals, raw), (nu_in, block_nu), (count_in, block_count)))
    ]
    mine = coef.at[pl.ds(group * chip + 3 * core, 3)]
    keep = pltpu.make_async_copy(
        shard.at[:, :, pl.ds(pl.multiple_of(width * core, 128), width)], mine, local_sems.at[3]
    )
    keep.start()
    for fetch in fetches:
        fetch.start()

    own_rows = pl.ds(pl.multiple_of(BLK * core, BLK), BLK)
    for fetch in fetches:
        fetch.wait()

    @pl.loop(0, mu_blocks)
    def _(m):
        relayout(raw, block_count[m], mats, m, pl.multiple_of(BLK * core, BLK))

    pl.semaphore_wait(barrier, 7)

    copies = []

    def send(src, dst, target):
        k = len(copies)
        copy = pltpu.make_async_remote_copy(
            src_ref=src, dst_ref=dst, send_sem=send_sems.at[k], recv_sem=recv_sems.at[k],
            device_id=target, device_id_type=MESH,
        )
        copy.start()
        copies.append(copy)
        return copy

    swap = send(shard.at[:, :, pl.ds(pl.multiple_of(width * (1 - core), 128), width)], mine, partner)

    parity = lax.rem(z, 2)

    class Stream:
        def __init__(self, offset, along_x, up):
            self.offset, self.along_x, self.up = offset, along_x, up
            self.plus, self.minus, self.far = {}, {}, {}

        def device(self, df, dg):
            return device(df, dg) if self.along_x else device(dg, df)

        def block(self, df, dg):
            dx, dy = (df, dg) if self.along_x else (dg, df)
            at_x = lax.rem(x + dx + SIDE, SIDE)
            at_y = lax.rem(y + dy + SIDE, SIDE)
            return coef.at[group * (at_x * SIDE + at_y) + self.offset]

        def first(self):
            block = self.block(0, 0)
            self.first_plus = send(block, block, self.device(1, 0))
            self.first_minus = send(block, block, self.device(-1, 0))

        def first_on(self):
            self.first_plus.wait_recv()
            low = self.block(-1, 0).at[pl.ds(0, BLK // 2)]
            self.far_low = send(low, low, self.device(1, 0))
            self.first_minus.wait_recv()
            high = self.block(1, 0).at[pl.ds(BLK // 2, BLK // 2)]
            self.far_high = send(high, high, self.device(-1, 0))

        def first_end(self):
            self.far_low.wait_recv()
            self.far_high.wait_recv()

        def second(self, df):
            block = self.block(df, 0)
            self.plus[df] = send(block, block, self.device(0, 1))
            self.minus[df] = send(block, block, self.device(0, -1))

        def second_on(self, df):
            self.plus[df].wait_recv()
            low = self.block(df, -1).at[pl.ds(0, BLK // 2)]
            low_copy = send(low, low, self.device(0, 1))
            self.minus[df].wait_recv()
            high = self.block(df, 1).at[pl.ds(BLK // 2, BLK // 2)]
            self.far[df] = (low_copy, send(high, high, self.device(0, -1)))

        def second_end(self, df):
            for copy in self.far[df]:
                copy.wait_recv()

        def beside(self, df, dg):
            if self.up:
                block = self.block(df, dg)
                from_beside.append(send(block, block, device(0, 0, self.up)))

    from_beside = []
    streams = [
        Stream(lax.rem(3 * core + 2 + 2 * parity, group), True, 1),
        Stream(lax.rem(3 * core + 3 + 2 * parity, group), False, -1),
        Stream(3 * core, True, 0),
        Stream(3 * core + 1, False, 0),
    ]
    def bring(begin, end):
        share = mats.at[pl.ds(begin, end - begin), own_rows]
        return send(share, share, partner)

    beside_streams, plain_streams = streams[:2], streams[2:]
    keep.wait()
    for stream in plain_streams:
        stream.first()
    swap.wait_recv()
    for stream in beside_streams:
        stream.first()
    for stream in beside_streams:
        stream.second(0)
    for stream in beside_streams:
        stream.first_on()
        stream.beside(-1, 0)
        stream.beside(1, 0)
    for stream in beside_streams:
        stream.second(-1)
    for stream in beside_streams:
        stream.second(1)
    mats_in = [bring(0, mu_blocks)]
    for stream in beside_streams:
        stream.first_end()
        stream.beside(2, 0)
    for stream in beside_streams:
        stream.second(2)
    for stream in beside_streams:
        stream.second_on(0)
        stream.beside(0, -1)
        stream.beside(0, 1)
    for stream in plain_streams:
        stream.second(0)
    for stream in plain_streams:
        stream.first_on()
        stream.beside(-1, 0)
        stream.beside(1, 0)
    for stream in plain_streams:
        stream.second(-1)
    for stream in plain_streams:
        stream.second(1)
    for stream in beside_streams:
        stream.second_on(-1)
        stream.beside(-1, -1)
        stream.beside(-1, 1)
    for stream in beside_streams:
        stream.second_end(0)
        stream.beside(0, 2)
    for stream in plain_streams:
        stream.first_end()
        stream.beside(2, 0)
    for stream in plain_streams:
        stream.second(2)
    for stream in beside_streams:
        stream.second_on(1)
        stream.beside(1, -1)
        stream.beside(1, 1)
    for stream in beside_streams:
        stream.second_end(-1)
        stream.beside(-1, 2)
    for stream in plain_streams:
        stream.second_on(0)
        stream.beside(0, -1)
        stream.beside(0, 1)
    for stream in beside_streams:
        stream.second_on(2)
        stream.beside(2, -1)
        stream.beside(2, 1)
    for stream in beside_streams:
        stream.second_end(1)
        stream.beside(1, 2)
    for stream in plain_streams:
        stream.second_on(-1)
        stream.beside(-1, -1)
        stream.beside(-1, 1)
    for stream in beside_streams:
        stream.second_end(2)
        stream.beside(2, 2)
    for stream in plain_streams:
        stream.second_on(1)
        stream.beside(1, -1)
        stream.beside(1, 1)
    for stream in plain_streams:
        stream.second_on(2)
        stream.beside(2, -1)
        stream.beside(2, 1)
    for stream in plain_streams:
        stream.second_end(0)
        stream.beside(0, 2)
    for stream in plain_streams:
        stream.second_end(-1)
        stream.beside(-1, 2)
    for stream in plain_streams:
        stream.second_end(1)
        stream.beside(1, 2)
    for stream in plain_streams:
        stream.second_end(2)
        stream.beside(2, 2)
    for copy in from_beside:
        copy.wait_recv()

    own_first = mu_blocks * z
    other_in = send(coef.at[pl.ds(own_first, mu_blocks)], other, partner)
    per_core = 4

    def place(rows, at_core):
        for q in range(per_core):
            turned_rows[per_core * at_core + q] = rows[160 * q : 160 * (q + 1)]

    place(turned(coef, own_first), core)
    for copy in mats_in:
        copy.wait_recv()

    @pl.loop(0, mu_blocks, unroll=4)
    def _(m):
        picked = jnp.concatenate([coef[block_nu[m, k]] for k in range(raw.shape[1])], axis=0)
        product = jnp.dot(mats[m], picked, preferred_element_type=jnp.float32)
        rows = pl.ds(pl.multiple_of(m * BLK, BLK), BLK)
        half[0, rows, :] = product[:BLK].astype(jnp.bfloat16)
        half[1, rows, :] = product[BLK:].astype(jnp.bfloat16)

    other_in.wait_recv()
    place(turned(other, 0), 1 - core)

    gathered = tuple(copies)

    def partial_sum(part, target, p):
        first, count = PARTS[part]
        return jnp.dot(
            turned_rows[target, first : first + count, :], half[p], preferred_element_type=jnp.float32
        )

    rings = [[[], []] for _ in PARTS]

    def ring_step(part, k):
        distance = 4 - (k + 1) // 2
        for way in range(2):
            ring = rings[part][way]
            p = k % 2 if way == 0 else 1 - k % 2
            step = distance if way == 0 else -distance
            value = partial_sum(part, lax.rem(z + step + depth, depth), p)
            if k >= 2:
                ring[k - 2].wait_recv()
                value = value + incoming[part][way, k - 2].astype(jnp.float32)
            outgoing[part][way, k] = value.astype(jnp.bfloat16)
            ring.append(
                send(
                    outgoing[part].at[way, k], incoming[part].at[way, k], device(0, 0, 1 if way == 0 else -1)
                )
            )

    def ring_end(part):
        count = PARTS[part][1]
        own = [partial_sum(part, z, p) for p in range(2)]
        final = finals[part]
        for way in range(2):
            for k in (5, 6):
                rings[part][way][k].wait_recv()
        for p in range(2):
            up, down = (6, 5) if p == 0 else (5, 6)
            value = own[p] + incoming[part][0, up].astype(jnp.float32)
            final[count * p : count * (p + 1), :] = value + incoming[part][1, down].astype(jnp.float32)
        if 2 * count < final.shape[0]:
            final[2 * count :, :] = jnp.zeros((final.shape[0] - 2 * count, width), jnp.float32)
        flips[part][...] = jnp.transpose(final[...], (1, 0))

    def last_copy(part, t):
        src = flips[part].at[pl.ds(pl.multiple_of(40 * t, 8), 40)]
        dst = landed[part].at[chip]
        owner = 16 * core + t

        def remote():
            return pltpu.make_async_remote_copy(
                src_ref=src, dst_ref=dst, send_sem=last_send.at[part, t], recv_sem=last_recv.at[part, chip],
                device_id=(owner, z), device_id_type=MESH,
            )

        return owner, remote, lambda: pltpu.make_async_copy(src, dst, last_recv.at[part, chip])

    own_place = lax.rem(me, 16)

    def give(part):
        @pl.loop(1, 16)
        def _(i):
            last_copy(part, lax.rem(own_place + i, 16))[1]().start()

        owner, remote, here = last_copy(part, own_place)

        @pl.when(owner == me)
        def _():
            here().start()

        @pl.when(owner != me)
        def _():
            remote().start()

    writes = []

    def take(part):
        first, count = PARTS[part]
        for s in range(16):
            block = landed[part].at[s]
            pltpu.make_async_copy(block, block, last_recv.at[part, s]).wait()
            for p in range(2):
                out[2 * s + p, :, first : first + count] = landed[part][s, :, count * p : count * (p + 1)]
            if part == len(PARTS) - 1:
                pair = pl.ds(2 * s, 2)
                done = pltpu.make_async_copy(out.at[pair], result.at[pair], out_sems.at[s])
                done.start()
                writes.append(done)

    for part, k in (
        (0, 0), (0, 1), (0, 2), (1, 0), (0, 3), (1, 1), (0, 4), (1, 2), (0, 5), (1, 3), (0, 6), (1, 4), (1, 5),
    ):
        ring_step(part, k)
        if (part, k) == (0, 3):
            for copy in gathered:
                copy.wait_send()
    ring_end(0)
    give(0)
    ring_step(1, 6)
    take(0)
    ring_end(1)
    give(1)
    take(1)

    for copy in copies[len(gathered) :]:
        copy.wait_send()
    for done in writes:
        done.wait()

    for part in range(len(PARTS)):

        @pl.loop(1, 16)
        def _(i):
            last_copy(part, lax.rem(own_place + i, 16))[1]().wait_send()

        owner, remote, _ = last_copy(part, own_place)

        @pl.when(owner != me)
        def _():
            remote().wait_send()


def local(depth, integrals, coefficients, block_nu, block_count):
    mu_blocks, slots, _, area = integrals.shape
    rows, orbitals = coefficients.shape
    width = orbitals // 2
    blocks = 96
    bf16, f32 = jnp.bfloat16, jnp.float32
    messages = 160
    return pl.pallas_call(
        functools.partial(kernel, depth),
        out_shape=jax.ShapeDtypeStruct((32, 40, 160), f32),
        in_specs=[
            pl.BlockSpec(memory_space=pl.ANY),
            pl.BlockSpec(memory_space=pl.ANY),
            pl.BlockSpec(memory_space=pl.ANY),
            pl.BlockSpec(memory_space=pl.ANY),
        ],
        out_specs=pl.BlockSpec(memory_space=pl.ANY),
        scratch_shapes=[
            pltpu.VMEM((32, 40, 160), f32),
            pltpu.VMEM((mu_blocks, slots, area), bf16),
            pltpu.SMEM((mu_blocks, slots), jnp.int32),
            pltpu.SMEM((mu_blocks,), jnp.int32),
            pltpu.VMEM((blocks, BLK, width), bf16),
            pltpu.VMEM((mu_blocks, 2 * BLK, slots * BLK), bf16),
            pltpu.VMEM((mu_blocks, BLK, width), bf16),
            pltpu.VMEM((8, 160, mu_blocks * BLK), bf16),
            pltpu.VMEM((2, mu_blocks * BLK, width), bf16),
            [pltpu.VMEM((2, 7, count, width), bf16) for _, count in PARTS],
            [pltpu.VMEM((2, 7, count, width), bf16) for _, count in PARTS],
            [pltpu.VMEM((lanes, width), f32) for lanes in (256, 128)],
            [pltpu.VMEM((width, lanes), f32) for lanes in (256, 128)],
            [pltpu.VMEM((16, 40, lanes), f32) for lanes in (256, 128)],
            pltpu.SemaphoreType.DMA((4,)),
            pltpu.SemaphoreType.DMA((16,)),
            pltpu.SemaphoreType.DMA((messages,)),
            pltpu.SemaphoreType.DMA((messages,)),
            pltpu.SemaphoreType.DMA((len(PARTS), 16)),
            pltpu.SemaphoreType.DMA((len(PARTS), 16)),
        ],
        compiler_params=pltpu.CompilerParams(
            collective_id=0, has_side_effects=True, vmem_limit_bytes=60 * 1024 * 1024
        ),
        cost_estimate=pl.CostEstimate(flops=6_000_000_000, bytes_accessed=4_000_000, transcendentals=0),
    )(
        integrals.reshape(mu_blocks, slots, area),
        coefficients.reshape(rows // BLK, BLK, orbitals),
        block_nu,
        block_count,
    )


def solution(mesh):
    placed = (P("basis", None, "aux", None), P("aux", None), P("basis", None), P("basis"))
    return jax.shard_map(
        functools.partial(local, mesh.shape["basis"]),
        mesh=mesh,
        in_specs=placed,
        out_specs=P(None, "aux", "basis"),
        check_vma=False,
    )
```

```python
import functools

import jax
import jax.numpy as jnp
from jax import lax
from jax.experimental import pallas as pl
from jax.experimental.pallas import tpu as pltpu
from jax.sharding import PartitionSpec as P

BLK = 64
SIDE = 4
MESH = pl.DeviceIdType.MESH
PARTS = ((0, 96), (96, 64))


def relayout(raw, count, target, m, first_row):
    slots, area = raw.shape[1:]
    values = raw[m].astype(jnp.float32)
    slot_ids = lax.broadcasted_iota(jnp.int32, (slots, area), 0)
    values = jnp.where(slot_ids < count, values, 0.0)
    pairs = area // (2 * BLK)
    by_pair = jnp.stack([values[:, 2 * BLK * a : 2 * BLK * (a + 1)] for a in range(pairs)], axis=0)
    by_slot = jnp.swapaxes(by_pair, 0, 1)
    low = lax.broadcasted_iota(jnp.int32, (pairs, 2 * BLK), 1) < BLK
    for k in range(0, slots, 2):
        one, two = by_slot[k], by_slot[k + 1]
        even = jnp.where(low, one, pltpu.roll(two, BLK, 1))
        odd = jnp.where(low, pltpu.roll(one, BLK, 1), two)
        columns = slice(BLK * k, BLK * (k + 2))
        target[m, pl.ds(first_row, pairs), columns] = even.astype(jnp.bfloat16)
        target[m, pl.ds(first_row + pairs, pairs), columns] = odd.astype(jnp.bfloat16)


def turned(blocks, first_block):
    new = lax.broadcasted_iota(jnp.int32, (BLK, BLK), 1)
    old = lax.broadcasted_iota(jnp.int32, (BLK, BLK), 0)
    source = jnp.where(new < BLK // 2, 2 * new, 2 * new - BLK + 1)
    order = (old == source).astype(jnp.bfloat16)
    columns = [
        lax.dot_general(
            blocks[first_block + m], order, (((0,), (0,)), ((), ())), preferred_element_type=jnp.float32
        )
        for m in range(12)
    ]
    return jnp.concatenate(columns, axis=1).astype(jnp.bfloat16)


def kernel(
    depth, integrals, shard, nu_in, count_in, result,
    out, raw, block_nu, block_count, coef, mats, other, turned_rows, half, outgoing, incoming, finals, flips, landed,
    local_sems, out_sems, send_sems, recv_sems, last_send, last_recv,
):
    me = lax.axis_index("aux")
    z = lax.axis_index("basis")
    core = lax.rem(me, 2)
    chip = lax.div(me, 2)
    x = lax.div(chip, SIDE)
    y = lax.rem(chip, SIDE)
    width = coef.shape[2]
    mu_blocks = raw.shape[0]
    group = 6

    def device(dx, dy, dz=0, core_at=core):
        at_x = lax.rem(x + dx + SIDE, SIDE)
        at_y = lax.rem(y + dy + SIDE, SIDE)
        return ((at_x * SIDE + at_y) * 2 + core_at, lax.rem(z + dz + depth, depth))

    partner = device(0, 0, 0, 1 - core)

    barrier = pltpu.get_barrier_semaphore()
    for friend in (
        device(1, 0), device(-1, 0), device(0, 1), device(0, -1), device(0, 0, 1), device(0, 0, -1), partner,
    ):
        pl.semaphore_signal(barrier, inc=1, device_id=friend, device_id_type=MESH)

    fetches = [
        pltpu.make_async_copy(src, dst, local_sems.at[k])
        for k, (src, dst) in enumerate(((integrals, raw), (nu_in, block_nu), (count_in, block_count)))
    ]
    mine = coef.at[pl.ds(group * chip + 3 * core, 3)]
    keep = pltpu.make_async_copy(
        shard.at[:, :, pl.ds(pl.multiple_of(width * core, 128), width)], mine, local_sems.at[3]
    )
    keep.start()
    for fetch in fetches:
        fetch.start()

    own_rows = pl.ds(pl.multiple_of(BLK * core, BLK), BLK)
    for fetch in fetches:
        fetch.wait()

    @pl.loop(0, mu_blocks)
    def _(m):
        relayout(raw, block_count[m], mats, m, pl.multiple_of(BLK * core, BLK))

    pl.semaphore_wait(barrier, 7)

    copies = []

    def send(src, dst, target):
        k = len(copies)
        copy = pltpu.make_async_remote_copy(
            src_ref=src, dst_ref=dst, send_sem=send_sems.at[k], recv_sem=recv_sems.at[k],
            device_id=target, device_id_type=MESH,
        )
        copy.start()
        copies.append(copy)
        return copy

    swap = send(shard.at[:, :, pl.ds(pl.multiple_of(width * (1 - core), 128), width)], mine, partner)

    parity = lax.rem(z, 2)

    class Stream:
        def __init__(self, offset, along_x, up):
            self.offset, self.along_x, self.up = offset, along_x, up
            self.plus, self.minus, self.far = {}, {}, {}

        def device(self, df, dg):
            return device(df, dg) if self.along_x else device(dg, df)

        def block(self, df, dg):
            dx, dy = (df, dg) if self.along_x else (dg, df)
            at_x = lax.rem(x + dx + SIDE, SIDE)
            at_y = lax.rem(y + dy + SIDE, SIDE)
            return coef.at[group * (at_x * SIDE + at_y) + self.offset]

        def first(self):
            block = self.block(0, 0)
            self.first_plus = send(block, block, self.device(1, 0))
            self.first_minus = send(block, block, self.device(-1, 0))

        def first_on(self):
            self.first_plus.wait_recv()
            low = self.block(-1, 0).at[pl.ds(0, BLK // 2)]
            self.far_low = send(low, low, self.device(1, 0))
            self.first_minus.wait_recv()
            high = self.block(1, 0).at[pl.ds(BLK // 2, BLK // 2)]
            self.far_high = send(high, high, self.device(-1, 0))

        def first_end(self):
            self.far_low.wait_recv()
            self.far_high.wait_recv()

        def second(self, df):
            block = self.block(df, 0)
            self.plus[df] = send(block, block, self.device(0, 1))
            self.minus[df] = send(block, block, self.device(0, -1))

        def second_on(self, df):
            self.plus[df].wait_recv()
            low = self.block(df, -1).at[pl.ds(0, BLK // 2)]
            low_copy = send(low, low, self.device(0, 1))
            self.minus[df].wait_recv()
            high = self.block(df, 1).at[pl.ds(BLK // 2, BLK // 2)]
            self.far[df] = (low_copy, send(high, high, self.device(0, -1)))

        def second_end(self, df):
            for copy in self.far[df]:
                copy.wait_recv()

        def beside(self, df, dg):
            if self.up:
                block = self.block(df, dg)
                from_beside.append(send(block, block, device(0, 0, self.up)))

    from_beside = []
    streams = [
        Stream(lax.rem(3 * core + 2 + 2 * parity, group), True, 1),
        Stream(lax.rem(3 * core + 3 + 2 * parity, group), False, -1),
        Stream(3 * core, True, 0),
        Stream(3 * core + 1, False, 0),
    ]
    def bring(begin, end):
        share = mats.at[pl.ds(begin, end - begin), own_rows]
        return send(share, share, partner)

    beside_streams, plain_streams = streams[:2], streams[2:]
    keep.wait()
    for stream in plain_streams:
        stream.first()
    swap.wait_recv()
    for stream in beside_streams:
        stream.first()
    for stream in beside_streams:
        stream.second(0)
    for stream in beside_streams:
        stream.first_on()
        stream.beside(-1, 0)
        stream.beside(1, 0)
    for stream in beside_streams:
        stream.second(-1)
    for stream in beside_streams:
        stream.second(1)
    mats_in = [bring(0, mu_blocks)]
    for stream in beside_streams:
        stream.first_end()
        stream.beside(2, 0)
    for stream in beside_streams:
        stream.second(2)
    for stream in beside_streams:
        stream.second_on(0)
        stream.beside(0, -1)
        stream.beside(0, 1)
    for stream in plain_streams:
        stream.second(0)
    for stream in plain_streams:
        stream.first_on()
        stream.beside(-1, 0)
        stream.beside(1, 0)
    for stream in plain_streams:
        stream.second(-1)
    for stream in plain_streams:
        stream.second(1)
    for stream in beside_streams:
        stream.second_on(-1)
        stream.beside(-1, -1)
        stream.beside(-1, 1)
    for stream in beside_streams:
        stream.second_end(0)
        stream.beside(0, 2)
    for stream in plain_streams:
        stream.first_end()
        stream.beside(2, 0)
    for stream in plain_streams:
        stream.second(2)
    for stream in beside_streams:
        stream.second_on(1)
        stream.beside(1, -1)
        stream.beside(1, 1)
    for stream in beside_streams:
        stream.second_end(-1)
        stream.beside(-1, 2)
    for stream in plain_streams:
        stream.second_on(0)
        stream.beside(0, -1)
        stream.beside(0, 1)
    for stream in beside_streams:
        stream.second_on(2)
        stream.beside(2, -1)
        stream.beside(2, 1)
    for stream in beside_streams:
        stream.second_end(1)
        stream.beside(1, 2)
    for stream in plain_streams:
        stream.second_on(-1)
        stream.beside(-1, -1)
        stream.beside(-1, 1)
    for stream in beside_streams:
        stream.second_end(2)
        stream.beside(2, 2)
    for stream in plain_streams:
        stream.second_on(1)
        stream.beside(1, -1)
        stream.beside(1, 1)
    for stream in plain_streams:
        stream.second_on(2)
        stream.beside(2, -1)
        stream.beside(2, 1)
    for stream in plain_streams:
        stream.second_end(0)
        stream.beside(0, 2)
    for stream in plain_streams:
        stream.second_end(-1)
        stream.beside(-1, 2)
    for stream in plain_streams:
        stream.second_end(1)
        stream.beside(1, 2)
    for stream in plain_streams:
        stream.second_end(2)
        stream.beside(2, 2)
    for copy in from_beside:
        copy.wait_recv()

    own_first = mu_blocks * z
    other_in = send(coef.at[pl.ds(own_first, mu_blocks)], other, partner)
    per_core = 4

    def place(rows, at_core):
        for q in range(per_core):
            turned_rows[per_core * at_core + q] = rows[160 * q : 160 * (q + 1)]

    place(turned(coef, own_first), core)
    for copy in mats_in:
        copy.wait_recv()

    @pl.loop(0, mu_blocks, unroll=4)
    def _(m):
        picked = jnp.concatenate([coef[block_nu[m, k]] for k in range(raw.shape[1])], axis=0)
        product = jnp.dot(mats[m], picked, preferred_element_type=jnp.float32)
        rows = pl.ds(pl.multiple_of(m * BLK, BLK), BLK)
        half[0, rows, :] = product[:BLK].astype(jnp.bfloat16)
        half[1, rows, :] = product[BLK:].astype(jnp.bfloat16)

    other_in.wait_recv()
    place(turned(other, 0), 1 - core)

    gathered = tuple(copies)

    def partial_sum(part, target, p):
        first, count = PARTS[part]
        return jnp.dot(
            turned_rows[target, first : first + count, :], half[p], preferred_element_type=jnp.float32
        )

    rings = [[[], []] for _ in PARTS]

    def ring_step(part, k):
        distance = 4 - (k + 1) // 2
        for way in range(2):
            ring = rings[part][way]
            p = k % 2 if way == 0 else 1 - k % 2
            step = distance if way == 0 else -distance
            value = partial_sum(part, lax.rem(z + step + depth, depth), p)
            if k >= 2:
                ring[k - 2].wait_recv()
                value = value + incoming[part][way, k - 2].astype(jnp.float32)
            outgoing[part][way, k] = value.astype(jnp.bfloat16)
            ring.append(
                send(
                    outgoing[part].at[way, k], incoming[part].at[way, k], device(0, 0, 1 if way == 0 else -1)
                )
            )

    def ring_end(part):
        count = PARTS[part][1]
        own = [partial_sum(part, z, p) for p in range(2)]
        final = finals[part]
        for way in range(2):
            for k in (5, 6):
                rings[part][way][k].wait_recv()
        for p in range(2):
            up, down = (6, 5) if p == 0 else (5, 6)
            value = own[p] + incoming[part][0, up].astype(jnp.float32)
            final[count * p : count * (p + 1), :] = value + incoming[part][1, down].astype(jnp.float32)
        if 2 * count < final.shape[0]:
            final[2 * count :, :] = jnp.zeros((final.shape[0] - 2 * count, width), jnp.float32)
        flips[part][...] = jnp.transpose(final[...], (1, 0))

    def last_copy(part, t):
        src = flips[part].at[pl.ds(pl.multiple_of(40 * t, 8), 40)]
        dst = landed[part].at[chip]
        owner = 16 * core + t

        def remote():
            return pltpu.make_async_remote_copy(
                src_ref=src, dst_ref=dst, send_sem=last_send.at[part, t], recv_sem=last_recv.at[part, chip],
                device_id=(owner, z), device_id_type=MESH,
            )

        return owner, remote, lambda: pltpu.make_async_copy(src, dst, last_recv.at[part, chip])

    own_place = lax.rem(me, 16)

    def give(part):
        @pl.loop(1, 16)
        def _(i):
            last_copy(part, lax.rem(own_place + i, 16))[1]().start()

        owner, remote, here = last_copy(part, own_place)

        @pl.when(owner == me)
        def _():
            here().start()

        @pl.when(owner != me)
        def _():
            remote().start()

    writes = []

    def take(part):
        first, count = PARTS[part]
        for s in range(16):
            block = landed[part].at[s]
            pltpu.make_async_copy(block, block, last_recv.at[part, s]).wait()
            for p in range(2):
                out[2 * s + p, :, first : first + count] = landed[part][s, :, count * p : count * (p + 1)]
            if part == len(PARTS) - 1:
                pair = pl.ds(2 * s, 2)
                done = pltpu.make_async_copy(out.at[pair], result.at[pair], out_sems.at[s])
                done.start()
                writes.append(done)

    for part, k in (
        (0, 0), (0, 1), (0, 2), (0, 3), (0, 4), (1, 0), (0, 5), (1, 1), (0, 6), (1, 2), (1, 3),
    ):
        ring_step(part, k)
        if (part, k) == (0, 3):
            for copy in gathered:
                copy.wait_send()
    ring_end(0)
    give(0)
    for k in (4, 5, 6):
        ring_step(1, k)
    take(0)
    ring_end(1)
    give(1)
    take(1)

    for copy in copies[len(gathered) :]:
        copy.wait_send()
    for done in writes:
        done.wait()

    for part in range(len(PARTS)):

        @pl.loop(1, 16)
        def _(i):
            last_copy(part, lax.rem(own_place + i, 16))[1]().wait_send()

        owner, remote, _ = last_copy(part, own_place)

        @pl.when(owner != me)
        def _():
            remote().wait_send()


def local(depth, integrals, coefficients, block_nu, block_count):
    mu_blocks, slots, _, area = integrals.shape
    rows, orbitals = coefficients.shape
    width = orbitals // 2
    blocks = 96
    bf16, f32 = jnp.bfloat16, jnp.float32
    messages = 160
    return pl.pallas_call(
        functools.partial(kernel, depth),
        out_shape=jax.ShapeDtypeStruct((32, 40, 160), f32),
        in_specs=[
            pl.BlockSpec(memory_space=pl.ANY),
            pl.BlockSpec(memory_space=pl.ANY),
            pl.BlockSpec(memory_space=pl.ANY),
            pl.BlockSpec(memory_space=pl.ANY),
        ],
        out_specs=pl.BlockSpec(memory_space=pl.ANY),
        scratch_shapes=[
            pltpu.VMEM((32, 40, 160), f32),
            pltpu.VMEM((mu_blocks, slots, area), bf16),
            pltpu.SMEM((mu_blocks, slots), jnp.int32),
            pltpu.SMEM((mu_blocks,), jnp.int32),
            pltpu.VMEM((blocks, BLK, width), bf16),
            pltpu.VMEM((mu_blocks, 2 * BLK, slots * BLK), bf16),
            pltpu.VMEM((mu_blocks, BLK, width), bf16),
            pltpu.VMEM((8, 160, mu_blocks * BLK), bf16),
            pltpu.VMEM((2, mu_blocks * BLK, width), bf16),
            [pltpu.VMEM((2, 7, count, width), bf16) for _, count in PARTS],
            [pltpu.VMEM((2, 7, count, width), bf16) for _, count in PARTS],
            [pltpu.VMEM((lanes, width), f32) for lanes in (256, 128)],
            [pltpu.VMEM((width, lanes), f32) for lanes in (256, 128)],
            [pltpu.VMEM((16, 40, lanes), f32) for lanes in (256, 128)],
            pltpu.SemaphoreType.DMA((4,)),
            pltpu.SemaphoreType.DMA((16,)),
            pltpu.SemaphoreType.DMA((messages,)),
            pltpu.SemaphoreType.DMA((messages,)),
            pltpu.SemaphoreType.DMA((len(PARTS), 16)),
            pltpu.SemaphoreType.DMA((len(PARTS), 16)),
        ],
        compiler_params=pltpu.CompilerParams(
            collective_id=0, has_side_effects=True, vmem_limit_bytes=60 * 1024 * 1024
        ),
        cost_estimate=pl.CostEstimate(flops=6_000_000_000, bytes_accessed=4_000_000, transcendentals=0),
    )(
        integrals.reshape(mu_blocks, slots, area),
        coefficients.reshape(rows // BLK, BLK, orbitals),
        block_nu,
        block_count,
    )


def solution(mesh):
    placed = (P("basis", None, "aux", None), P("aux", None), P("basis", None), P("basis"))
    return jax.shard_map(
        functools.partial(local, mesh.shape["basis"]),
        mesh=mesh,
        in_specs=placed,
        out_specs=P(None, "aux", "basis"),
        check_vma=False,
    )
```
